128 devices in a mesh: fsdp: 8 (over x_lo, z), tp: 16 (over y, x_hi, core).
Axes of the slice: x: 4 (x_hi: 2, x_lo: 2; x = x_hi * 2 + x_lo), y: 4, z: 4, core: 2. Of those that a mesh axis runs over, the one named last changes fastest.
Arguments:
- tokens: bfloat16 [6016, 4096], P('fsdp', 'tp'), may hold values from -6 to 6
- norm_gain: float32 [4096], replicated, may hold values from 0.5 to 1.5
- base_gate: bfloat16 [4096, 12288], P(None, 'tp'), may hold values from -0.09375 to 0.09375
- base_up: bfloat16 [4096, 12288], P(None, 'tp'), may hold values from -0.09375 to 0.09375
- base_down: bfloat16 [12288, 4096], P('tp'), may hold values from -0.0546875 to 0.0546875
- code_gate: bfloat16 [4096, 12288], P(('fsdp', 'tp')), may hold values from -4 to 4
- code_up: bfloat16 [4096, 12288], P(('fsdp', 'tp')), may hold values from -4 to 4
- scale_gate: float32 [4096, 96], P(('fsdp', 'tp')), may hold values from 0.005 to 0.05
- scale_up: float32 [4096, 96], P(('fsdp', 'tp')), may hold values from 0.005 to 0.05
- code_down: bfloat16 [12288, 4096], P(None, ('fsdp', 'tp')), may hold values from -4 to 4
- scale_down: float32 [96, 4096], P(None, ('fsdp', 'tp')), may hold values from 0.005 to 0.05
- cu_seqlens: int32 [8, 9], P('fsdp'), may hold values from 0 to 752, as said below
Outputs:
- mixed: bfloat16 [6016, 4096], P('fsdp', 'tp')
- seq_means: float32 [64, 4096], P('fsdp', 'tp')
The draws below stay inside these ranges and needn't reach their ends.
Inputs may be any that keep to these rules, and one draw needn't show every extreme that they name: `cu_seqlens`: each row starts at 0 and rises strictly; its last entry is the group's live tokens, which fill the first slots of its 752. Over all groups the live tokens add up to exactly 3072, and some group has exactly 752.
All inputs are finite; a program needn't handle non-finite values.
Results may differ from the reference program's by a relative error of at most 0.023.
Values may be sent and summed in bfloat16 or wider, within the bound.
No kernel may reach another device: no remote copies, remote signals or barrier semaphores. Data moves between devices by JAX's collectives and lax.ppermute only.
A program may use at most 256 MiB of HBM per device.

```python
import math
import jax
import jax.numpy as jnp
from jax import lax

D = 4096
FF = 12288
BLK = 128
SEQS = 8
BAL = 384
CAP = 752
GROUPS = 8
TOKENS = 6016
N_TP = 16


def draw_cu_seqlens(key, part):
    key_pairs = jax.random.fold_in(key, 11)
    key_order = jax.random.fold_in(key, 12)
    key_cuts = jax.random.fold_in(key, 13)
    spread = jax.random.randint(key_pairs, (GROUPS // 2,), 0, BAL - 2 * SEQS + 1).astype(jnp.int32)
    spread = spread.at[0].set(BAL - 2 * SEQS)
    counts = jnp.stack([BAL + spread, BAL - spread], axis=1).reshape(GROUPS)
    counts = counts[jax.random.permutation(key_order, GROUPS)]
    upper_bound = (counts - SEQS + 1)[:, None]
    cut_points = jax.random.randint(key_cuts, (GROUPS, SEQS - 1), 0, upper_bound).astype(jnp.int32)
    cut_points = jnp.sort(cut_points, axis=1) + jnp.arange(1, SEQS, dtype=jnp.int32)[None, :]
    leading = jnp.zeros((GROUPS, 1), jnp.int32)
    return jnp.concatenate([leading, cut_points, counts[:, None].astype(jnp.int32)], axis=1)


def levels(key, dims, cuts, low, high):
    def one(axis_at, shards_of):
        steps = jax.random.uniform(jax.random.fold_in(jax.random.fold_in(key, 6), axis_at), (shards_of,), jnp.float32, low / len(cuts), high / len(cuts))
        return jnp.repeat(jnp.exp(steps), dims[axis_at] // shards_of).reshape((-1,) + (1,) * (len(dims) - axis_at - 1))

    factor_of = one(*cuts[0])
    for cut in cuts[1:]:
        factor_of = factor_of * one(*cut)
    return factor_of


def gaussian(key, dims, width, reach, shards=(), kind=jnp.bfloat16):
    values = jax.random.normal(key, dims, jnp.float32) * width
    if len(shards) > 0:
        values = levels(key, dims, shards, -0.22, 0.18) * values
    return jnp.clip(values, min=-reach, max=reach).astype(kind)


def setup_inputs(seed: int = 0) -> dict:
    seeds = jax.random.split(jax.random.key(seed), 13)
    tokens = gaussian(seeds[0], (TOKENS, D), 1.0, 6.0, ((0, 8), (1, 16)))
    norm_gain = jnp.clip(jax.random.uniform(seeds[1], (D,), jnp.float32, 0.5, 1.5), 0.5, 1.5)
    base_gate = gaussian(seeds[2], (D, FF), D ** -0.5, 0.09375, ((1, 16),))
    base_up = gaussian(seeds[3], (D, FF), D ** -0.5, 0.09375, ((1, 16),))
    base_down = gaussian(seeds[4], (FF, D), FF ** -0.5, 0.0546875, ((0, 16),))
    code_gate = gaussian(seeds[5], (D, FF), 1.0, 4.0, ((0, 128),))
    code_up = gaussian(seeds[6], (D, FF), 1.0, 4.0, ((0, 128),))
    scale_gate = jnp.clip(jnp.exp(math.log(0.05) - 2.3025851 * jax.random.uniform(seeds[7], (D, FF // BLK), jnp.float32) ** levels(seeds[7], (D, FF // BLK), ((0, 128),), -0.2, 0.2)), 0.005, 0.05)
    scale_up = jnp.clip(jnp.exp(math.log(0.05) - 2.3025851 * jax.random.uniform(seeds[8], (D, FF // BLK), jnp.float32) ** levels(seeds[8], (D, FF // BLK), ((0, 128),), -0.2, 0.2)), 0.005, 0.05)
    code_down = gaussian(seeds[9], (FF, D), 1.0, 4.0, ((1, 128),))
    scale_down = jnp.clip(jnp.exp(math.log(0.05) - 2.3025851 * jax.random.uniform(seeds[10], (FF // BLK, D), jnp.float32) ** levels(seeds[10], (FF // BLK, D), ((1, 128),), -0.2, 0.2)), 0.005, 0.05)
    cu_seqlens = draw_cu_seqlens(jax.random.fold_in(seeds[12], 71), 0)
    return {"tokens": tokens, "norm_gain": norm_gain, "base_gate": base_gate, "base_up": base_up, "base_down": base_down, "code_gate": code_gate, "code_up": code_up, "scale_gate": scale_gate, "scale_up": scale_up, "code_down": code_down, "scale_down": scale_down, "cu_seqlens": cu_seqlens}


EPSILON = 1e-06

def reference(tokens, norm_gain, base_gate, base_up, base_down, code_gate, code_up, scale_gate, scale_up, code_down, scale_down, cu_seqlens):
    w_gate = (base_gate.astype(jnp.float32) + code_gate.astype(jnp.float32) * jnp.repeat(scale_gate, BLK, axis=1)).astype(jnp.bfloat16)
    w_up = (base_up.astype(jnp.float32) + code_up.astype(jnp.float32) * jnp.repeat(scale_up, BLK, axis=1)).astype(jnp.bfloat16)
    w_down = (base_down.astype(jnp.float32) + code_down.astype(jnp.float32) * jnp.repeat(scale_down, BLK, axis=0)).astype(jnp.bfloat16)
    slice_width = FF // N_TP
    down_slices = w_down.reshape(N_TP, slice_width, D)
    stacked = tokens.reshape(GROUPS, CAP, D)
    positions = jnp.arange(CAP, dtype=jnp.int32)

    def one_group(operands):
        rows_in, bounds = operands
        widened = rows_in.astype(jnp.float32)
        inverse = lax.rsqrt(lax.optimization_barrier(jnp.mean(widened * widened, axis=1, keepdims=True)) + EPSILON)
        normed = (widened * inverse * norm_gain[None, :]).astype(jnp.bfloat16)
        gate_out = jnp.dot(normed, w_gate, preferred_element_type=jnp.float32)
        up_out = jnp.dot(normed, w_up, preferred_element_type=jnp.float32)
        hidden = (jax.nn.silu(gate_out) * up_out).astype(jnp.bfloat16)
        hidden_slices = hidden.reshape(CAP, N_TP, slice_width).transpose(1, 0, 2)

        def add_slice(running, pair):
            partial_value = jnp.dot(pair[0], pair[1], preferred_element_type=jnp.float32).astype(jnp.bfloat16)
            return (running + partial_value.astype(jnp.float32), None)
        summed, _ = lax.scan(add_slice, jnp.zeros((CAP, D), jnp.float32), (hidden_slices, down_slices))
        mixed_rows = (widened + summed).astype(jnp.bfloat16)
        live_count = bounds[SEQS]
        mixed_rows = jnp.where((positions < live_count)[:, None], mixed_rows, jnp.zeros((), jnp.bfloat16))
        member = (positions[None, :] >= bounds[:-1, None]) & (positions[None, :] < bounds[1:, None])
        seq_sums = jnp.dot(member.astype(jnp.bfloat16), mixed_rows, preferred_element_type=jnp.float32)
        lengths = (bounds[1:] - bounds[:-1]).astype(jnp.float32)
        return (mixed_rows, seq_sums / lengths[:, None])
    mixed_all, means_all = lax.map(one_group, (stacked, cu_seqlens))
    return (mixed_all.reshape(GROUPS * CAP, D), means_all.reshape(GROUPS * SEQS, D))
```

```python
import jax
import jax.numpy as jnp
from jax import lax
from jax.experimental import pallas as pl
from jax.experimental.pallas import tpu as pltpu
from jax.sharding import Mesh
from jax.sharding import PartitionSpec as P

SEQS = 8
EPSILON = 1e-06
HALF_A = 384
PLANE = ("xl", "y", "xh", "c")
BF = jnp.bfloat16
F32 = jnp.float32
VMEM = pl.BlockSpec(memory_space=pltpu.VMEM)
SMEM = pl.BlockSpec(memory_space=pltpu.SMEM)


def ring_pairs(size, chip_index):
    pairs = []
    for core in range(2):
        for place in range(size):
            there = (place + (1 if core == 0 else -1)) % size
            pairs.append((chip_index(place) * 2 + core, chip_index(there) * 2 + core))
    return pairs


def step_z(value):
    return lax.ppermute(value, ("z", "c"), ring_pairs(4, lambda p: p))


def step_y(value):
    return lax.ppermute(value, ("y", "c"), ring_pairs(4, lambda p: p))


def step_x(value):
    return lax.ppermute(value, ("xl", "xh", "c"), ring_pairs(4, lambda p: (p % 2) * 2 + p // 2))


def swap_cores(value):
    return lax.ppermute(value, "c", [(0, 1), (1, 0)])


def ring_gather(value, step):
    pieces = [value]
    for _ in range(3):
        pieces.append(step(pieces[-1]))
    return pieces


def to_units(delta):
    rows, units = delta.shape
    parts = delta.reshape(rows, 16, 2, units // 32).transpose(2, 1, 0, 3)
    parts = parts.reshape(32, rows, units // 32)
    moved = lax.all_to_all(parts, PLANE, split_axis=0, concat_axis=0, tiled=True)
    return moved.reshape(32 * rows, units // 32)


def scaled_rows(code, scale):
    rows, units = code.shape
    blocks = scale.shape[1]
    spread = code.astype(F32).reshape(rows, blocks, units // blocks) * scale[:, :, None]
    return spread.reshape(rows, units).astype(BF)


def project(table, base, deltas, gain, pieces_a, pieces_b, w, acc, visit):
    for s in range(4):
        z_s = table[s]
        for xl in range(2):
            at = pl.multiple_of(xl * 2048 + z_s * 512, 512)
            total = base[pl.ds(at, 512), :].astype(F32)
            total += deltas[s][xl * 512 : (xl + 1) * 512, :].astype(F32)
            factor = gain[pl.ds(at, 512), :]
            w[pl.ds(at, 512), :] = (total * jnp.concatenate([factor] * 3, axis=1)).astype(BF)
    acc[...] = jnp.zeros_like(acc)
    for core in range(2):
        x_at, y_at = 4 + 8 * core, 8 + 8 * core
        for group in range(4):
            x_g = table[x_at + group]
            part = None
            for s in range(4):
                unit = table[y_at + s] * 4 + (x_g // 2) * 2 + table[20 + core]
                weights = w[pl.ds(pl.multiple_of(unit * 256, 256), 256), :]
                block = pieces_a[core][group][s]
                visit(x_g % 2, 0, block)
                term = jnp.dot(block, weights, preferred_element_type=F32)
                part = term if part is None else part + term
            acc[x_g % 2, :HALF_A, :] += part
            part = None
            for s in range(4):
                unit = table[y_at + s] * 4 + (x_g // 2) * 2 + table[20 + core]
                weights = w[pl.ds(pl.multiple_of(unit * 256, 256), 256), :]
                block = pieces_b[core][s][group]
                visit(x_g % 2, HALF_A, block)
                term = jnp.dot(block, weights, preferred_element_type=F32)
                part = term if part is None else part + term
            acc[x_g % 2, HALF_A:, :] += part


def split_refs(refs):
    base, gain = refs[0], refs[1]
    deltas = refs[2:6]
    pieces_a = (refs[6:10], refs[10:14])
    pieces_b = (refs[14:18], refs[18:22])
    return base, gain, deltas, pieces_a, pieces_b, refs[22:]


def gate_kernel(table, *refs):
    base, gain, deltas, pieces_a, pieces_b, rest = split_refs(refs)
    out, inverse, w, acc, squares = rest
    squares[...] = jnp.zeros_like(squares)

    def visit(xl, start, block):
        wide = block.astype(F32)
        wide = wide * wide
        squares[xl, start : start + block.shape[0], :] += wide[:, :128] + wide[:, 128:]

    project(table, base, deltas, gain, pieces_a, pieces_b, w, acc, visit)
    for xl in range(2):
        mean = jnp.sum(squares[xl], axis=1, keepdims=True) * (1.0 / 4096.0)
        inv = lax.rsqrt(mean + EPSILON)
        inverse[xl] = jnp.broadcast_to(inv, inverse.shape[1:])
        gate = acc[xl] * inv
        out[xl] = gate / (1.0 + jnp.exp(-gate))


def up_kernel(table, *refs):
    base, gain, deltas, pieces_a, pieces_b, rest = split_refs(refs)
    silu, inverse, out, w, acc = rest
    project(table, base, deltas, gain, pieces_a, pieces_b, w, acc, lambda *_: None)
    for xl in range(2):
        inv = jnp.concatenate([inverse[xl]] * 3, axis=1)
        out[xl] = (silu[xl] * (acc[xl] * inv)).astype(BF)


def down_weights_kernel(table, base, d0, d1, d2, d3, out):
    for s, delta in enumerate((d0, d1, d2, d3)):
        for xl in range(2):
            for half in range(2):
                unit = xl * 8 + table[s] * 2 + half
                at = pl.multiple_of(unit * 256, 256)
                first = xl * 512 + half * 256
                total = base[:, pl.ds(at, 256)].astype(F32)
                total += delta[:, first : first + 256].astype(F32)
                out[unit] = total.astype(BF)


def down_kernel(table, hidden, w, out_a, out_b):
    part = jnp.dot(hidden[0], w[0], preferred_element_type=F32).astype(BF)
    out_a[0, 0] = part[:HALF_A]
    out_b[0, 0] = part[HALF_A:]


PARAMS = pltpu.CompilerParams(vmem_limit_bytes=56 * 1024 * 1024)


def down_partials(table, hidden, w):
    rows = hidden.shape[1]
    grid_spec = pltpu.PrefetchScalarGridSpec(
        num_scalar_prefetch=1,
        grid=(4, 4),
        in_specs=[
            pl.BlockSpec((1, rows, 384), lambda i, j, t: (t[i] % 2, 0, 0)),
            pl.BlockSpec((1, 384, 256), lambda i, j, t: (t[4 + j] * 4 + (t[i] // 2) * 2 + t[8], 0, 0)),
        ],
        out_specs=[
            pl.BlockSpec((1, 1, HALF_A, 256), lambda i, j, t: (i, j, 0, 0)),
            pl.BlockSpec((1, 1, rows - HALF_A, 256), lambda i, j, t: (j, i, 0, 0)),
        ],
    )
    return pl.pallas_call(
        down_kernel,
        grid_spec=grid_spec,
        out_shape=[
            jax.ShapeDtypeStruct((4, 4, HALF_A, 256), BF),
            jax.ShapeDtypeStruct((4, 4, rows - HALF_A, 256), BF),
        ],
        compiler_params=PARAMS,
    )(table, hidden, w)


def add(*parts):
    total = parts[0].astype(F32)
    for part in parts[1:]:
        total = total + part.astype(F32)
    return total


def ring_scatter(kept, crossed, first, second):
    moving = add(kept[0], crossed[0]).astype(BF)
    for s in range(1, 4):
        moving = add(first(moving), kept[s], crossed[s]).astype(BF)
    running = moving[0]
    for s in range(1, 4):
        running = add(second(running), moving[s])
        if s < 3:
            running = running.astype(BF)
    return running


def shards(
    tokens,
    norm_gain,
    base_gate,
    base_up,
    base_down,
    code_gate,
    code_up,
    scale_gate,
    scale_up,
    code_down,
    scale_down,
    cu_seqlens,
):
    capacity = tokens.shape[0]
    rows_b = capacity - HALF_A
    xl, z, y, xh, c = (lax.axis_index(a) for a in ("xl", "z", "y", "xh", "c"))
    x = xh * 2 + xl
    four = jnp.arange(4, dtype=jnp.int32)
    way = 1 - 2 * c

    delta_gate = to_units(scaled_rows(code_gate, scale_gate))
    delta_up = to_units(scaled_rows(code_up, scale_up))
    turned = lax.dot_general(
        jnp.eye(32, dtype=BF), code_down, (((1,), (1,)), ((), ())), preferred_element_type=F32
    )
    delta_down = to_units(scaled_rows(turned, scale_down.T)).T

    gates = ring_gather(delta_gate, step_z)
    ups = ring_gather(delta_up, step_z)
    downs = ring_gather(delta_down, step_z)

    stack_a = jnp.stack(ring_gather(tokens[:HALF_A], step_y))
    stack_b = jnp.stack(ring_gather(tokens[HALF_A:], step_x))
    mine_a = ring_gather(stack_a, step_x)
    mine_b = ring_gather(stack_b, step_y)
    other_a = [swap_cores(v) for v in mine_a]
    other_b = [swap_cores(v) for v in mine_b]
    z_order = (z - way * four) % 4

    def orders(w):
        return [(x - w * four) % 4, (y - w * four) % 4]

    table = jnp.concatenate(
        [z_order] + orders(way) + orders(-way) + [jnp.stack([c, 1 - c])]
    ).astype(jnp.int32)
    gain = jnp.broadcast_to(norm_gain[:, None], (norm_gain.shape[0], 128))
    width = base_gate.shape[1] // 2
    half_gate = lax.dynamic_slice_in_dim(base_gate, xl * width, width, axis=1)
    half_up = lax.dynamic_slice_in_dim(base_up, xl * width, width, axis=1)
    half_down = lax.dynamic_slice_in_dim(base_down, xl * width, width, axis=0)
    pieces = (*mine_a, *other_a, *mine_b, *other_b)

    silu, inverse = pl.pallas_call(
        gate_kernel,
        in_specs=[SMEM] + [VMEM] * 22,
        out_specs=[VMEM] * 2,
        out_shape=[
            jax.ShapeDtypeStruct((2, capacity, width), F32),
            jax.ShapeDtypeStruct((2, capacity, 128), F32),
        ],
        scratch_shapes=[
            pltpu.VMEM((4096, width), BF),
            pltpu.VMEM((2, capacity, width), F32),
            pltpu.VMEM((2, capacity, 128), F32),
        ],
        compiler_params=PARAMS,
    )(table, half_gate, gain, *gates, *pieces)
    hidden = pl.pallas_call(
        up_kernel,
        in_specs=[SMEM] + [VMEM] * 24,
        out_specs=VMEM,
        out_shape=jax.ShapeDtypeStruct((2, capacity, width), BF),
        scratch_shapes=[
            pltpu.VMEM((4096, width), BF),
            pltpu.VMEM((2, capacity, width), F32),
        ],
        compiler_params=PARAMS,
    )(table, half_up, gain, *ups, *pieces, silu, inverse)

    w_down = pl.pallas_call(
        down_weights_kernel,
        in_specs=[SMEM] + [VMEM] * 5,
        out_specs=VMEM,
        out_shape=jax.ShapeDtypeStruct((16, width, 256), BF),
        compiler_params=PARAMS,
    )(table, half_down, *downs)

    def down_table(core):
        w = 1 - 2 * core
        return jnp.concatenate(
            [(x - w * (four + 1)) % 4, (y - w * (four + 1)) % 4, core[None]]
        ).astype(jnp.int32)

    send_a, send_b = down_partials(down_table(1 - c), hidden, w_down)
    crossed_a, crossed_b = swap_cores(send_a), swap_cores(send_b)
    kept_a, kept_b = down_partials(down_table(c), hidden, w_down)
    sum_a = ring_scatter(kept_a, crossed_a, step_x, step_y)
    sum_b = ring_scatter(kept_b, crossed_b, step_y, step_x)
    summed = jnp.concatenate([sum_a, sum_b])

    bounds = cu_seqlens[0]
    positions = jnp.arange(capacity, dtype=jnp.int32)
    mixed = (tokens.astype(F32) + summed).astype(BF)
    mixed = jnp.where((positions < bounds[SEQS])[:, None], mixed, jnp.zeros((), BF))
    member = (positions[None, :] >= bounds[:-1, None]) & (positions[None, :] < bounds[1:, None])
    seq_sums = jnp.dot(member.astype(BF), mixed, preferred_element_type=F32)
    lengths = (bounds[1:] - bounds[:-1]).astype(F32)
    return (mixed, seq_sums / lengths[:, None])


def solution(mesh):
    torus = Mesh(mesh.devices.reshape(2, 4, 4, 2, 2), ("xl", "z", "y", "xh", "c"))
    fsdp, tp = ("xl", "z"), ("y", "xh", "c")
    both = fsdp + tp
    in_specs = (
        P(fsdp, tp),
        P(),
        P(None, tp),
        P(None, tp),
        P(tp, None),
        P(both, None),
        P(both, None),
        P(both, None),
        P(both, None),
        P(None, both),
        P(None, both),
        P(fsdp, None),
    )
    out_specs = (P(fsdp, tp), P(fsdp, tp))
    return jax.shard_map(shards, mesh=torus, in_specs=in_specs, out_specs=out_specs, check_vma=False)
```

```python
import jax
import jax.numpy as jnp
from jax import lax
from jax.experimental import pallas as pl
from jax.experimental.pallas import tpu as pltpu
from jax.sharding import Mesh
from jax.sharding import PartitionSpec as P

SEQS = 8
EPSILON = 1e-06
HALF_A = 384
PLANE = ("xl", "y", "xh", "c")
BF = jnp.bfloat16
F32 = jnp.float32
VMEM = pl.BlockSpec(memory_space=pltpu.VMEM)
SMEM = pl.BlockSpec(memory_space=pltpu.SMEM)


def ring_pairs(steps, chip_index):
    pairs = []
    for core in range(2):
        for place in range(4):
            there = (place + (steps if core == 0 else -steps)) % 4
            pairs.append((chip_index(place) * 2 + core, chip_index(there) * 2 + core))
    return pairs


def step_z(value, steps=1):
    return lax.ppermute(value, ("z", "c"), ring_pairs(steps, lambda p: p))


def step_y(value, steps=1):
    return lax.ppermute(value, ("y", "c"), ring_pairs(steps, lambda p: p))


def step_x(value, steps=1):
    order = ring_pairs(steps, lambda p: (p % 2) * 2 + p // 2)
    return lax.ppermute(value, ("xl", "xh", "c"), order)


def swap_cores(value):
    return lax.ppermute(value, "c", [(0, 1), (1, 0)])


def after(value, other):
    return lax.optimization_barrier((value, other))[0]


def ring_gather(value, step):
    pieces = [value]
    for _ in range(3):
        pieces.append(step(pieces[-1]))
    return pieces


def direct_gather(value, step):
    return [value] + [step(value, s) for s in (1, 2, 3)]


def by_units(*deltas):
    rows, units = deltas[0].shape
    count, width = len(deltas), units // 32
    parts = [d.reshape(rows, 16, 2, width).transpose(2, 1, 0, 3) for d in deltas]
    return jnp.stack(parts, axis=2).reshape(32, count, rows, width)


def to_units(parts):
    return lax.all_to_all(parts, PLANE, split_axis=0, concat_axis=0, tiled=True)


def scaled_rows(code, scale):
    rows, units = code.shape
    blocks = scale.shape[1]
    spread = code.astype(F32).reshape(rows, blocks, units // blocks) * scale[:, :, None]
    return spread.reshape(rows, units).astype(BF)


PARAMS = pltpu.CompilerParams(vmem_limit_bytes=60 * 1024 * 1024)


def cost(flops, bytes_accessed):
    return pl.CostEstimate(flops=int(flops), bytes_accessed=int(bytes_accessed), transcendentals=0)


def weights_kernel(table, base_gate, base_up, gain, d0, d1, d2, d3, out):
    width = base_gate.shape[1]
    for s, delta in enumerate((d0, d1, d2, d3)):
        for xl in range(2):
            for k in range(4):
                at = pl.multiple_of(xl * 2048 + table[s] * 512 + k * 128, 128)
                row = gain[pl.ds(at // 128, 1), :]
                factor = jnp.broadcast_to(row, (128, 128)).T
                factor = jnp.concatenate([factor] * 3, axis=1)
                first = xl * 16 + k * 4
                for which, base in enumerate((base_gate, base_up)):
                    total = base[pl.ds(at, 128), :].astype(F32)
                    total += delta[first : first + 4, which].reshape(128, width).astype(F32)
                    total = (total * factor).astype(BF)
                    out[pl.ds(at, 128), which * width : (which + 1) * width] = total


def hidden_kernel(table, w_from, *refs):
    pieces = ((refs[0:4], refs[4:8]), (refs[8:12], refs[12:16]))
    outs, halves, (w, inverse, done) = refs[16:18], refs[18:20], refs[20:]
    width = outs[0].shape[1]
    copies = ([], [])
    for half in range(2):
        for core in range(2):
            for i in range(4):
                for j in range(4):
                    x_i, y_j = table[4 + 8 * core + i], table[8 + 8 * core + j]
                    unit = y_j * 4 + (x_i // 2) * 2 + table[20 + core]
                    group = pieces[half][core]
                    copies[half].append(
                        pltpu.make_async_copy(
                            group[j].at[i] if half else group[i].at[j],
                            halves[half].at[
                                x_i % 2, :, pl.ds(pl.multiple_of(unit * 256, 256), 256)
                            ],
                            done.at[half * 32 + core * 16 + i * 4 + j],
                        )
                    )
    weights = pltpu.make_async_copy(w_from, w, done.at[64])
    for copy in copies[0]:
        copy.start()
    weights.start()
    for copy in copies[1]:
        copy.start()
    for half in range(2):
        rows, out = halves[half], outs[half]
        count = rows.shape[1]
        for copy in copies[half]:
            copy.wait()
        for xl in range(2):
            for first in range(0, count, 64):
                last = min(first + 64, count)
                total = jnp.zeros((last - first, 128), F32)
                for k in range(16):
                    wide = rows[xl, first:last, k * 256 : (k + 1) * 256].astype(F32)
                    wide = wide * wide
                    total += wide[:, :128] + wide[:, 128:]
                mean = jnp.sum(total, axis=1, keepdims=True) * (1.0 / 4096.0)
                value = lax.rsqrt(mean + EPSILON)
                inverse[first:last, :] = jnp.broadcast_to(value, (last - first, 128))
            if half == 0 and xl == 0:
                weights.wait()
            both = jnp.dot(rows[xl], w[...], preferred_element_type=F32)
            factor = jnp.concatenate([inverse[:count, :]] * 3, axis=1)
            gate = both[:, :width] * factor
            hidden = gate / (1.0 + jnp.exp(-gate)) * (both[:, width:] * factor)
            out[xl * count : (xl + 1) * count, :] = hidden.astype(BF)


def down_weights_kernel(table, base, *refs):
    *deltas, out = refs
    width = base.shape[0]
    for s, delta in enumerate(deltas):
        place = table[s]
        for xl in range(2):
            for core in range(2):
                at = pl.multiple_of((xl * 8 + place * 2 + core) * 256, 256)
                first = xl * 16 + core * 8
                total = base[:, pl.ds(at, 256)].astype(F32)
                total += delta[first : first + 8].reshape(256, width).astype(F32).T
                out[xl, place // 2, place % 2, core] = total.astype(BF)


def down_kernel(table, hidden_a, hidden_b, w, *outs):
    order = 35 + pl.num_programs(0) + 2 * pl.program_id(0)
    start, at = table[order], table[order + 1]
    rows_a, rows_b = outs[0].shape[2], outs[1].shape[2]
    x_i = table[start + at]
    left = hidden_a[pl.ds(pl.multiple_of((x_i % 2) * rows_a, rows_a), rows_a), :]
    right = jnp.concatenate([w[y // 2, y % 2, x_i // 2, 0] for y in range(4)], axis=1)
    part_a = jnp.dot(left, right, preferred_element_type=F32).astype(BF)
    y_j = table[start + 4 + at]
    right = jnp.concatenate([w[y_j // 2, y_j % 2, xh, 0] for xh in range(2)], axis=1)
    part_b = jnp.dot(hidden_b[...], right, preferred_element_type=F32).astype(BF)

    def write(out_a, out_b):
        for y in range(4):
            out_a[0, table[start + 8 + y]] = part_a[:, y * 256 : (y + 1) * 256]
        for xh in range(2):
            for xl in range(2):
                value = part_b[xl * rows_b : (xl + 1) * rows_b, xh * 256 : (xh + 1) * 256]
                out_b[0, table[start + 12 + xh * 2 + xl]] = value

    write(*outs)


def down_partials(table, hidden_a, hidden_b, w, chunks):
    rows_a, rows_b = hidden_a.shape[0] // 2, hidden_b.shape[0] // 2
    width = hidden_a.shape[1]
    steps = len(chunks)
    order = [value for place, step in chunks for value in (place * 17, step)] + [0, 0]
    cores = [table[place * 17 + 16] for place, _ in chunks] + [jnp.int32(0)]
    table = jnp.concatenate([table, jnp.stack(cores), jnp.array(order, jnp.int32)])
    whole = lambda g, t: (0, 0)
    grid_spec = pltpu.PrefetchScalarGridSpec(
        num_scalar_prefetch=1,
        grid=(steps,),
        in_specs=[
            pl.BlockSpec(hidden_a.shape, whole),
            pl.BlockSpec(hidden_b.shape, whole),
            pl.BlockSpec((2, 2, 2, 1, width, 256), lambda g, t: (0, 0, 0, t[34 + g], 0, 0)),
        ],
        out_specs=[
            pl.BlockSpec((1, 4, rows, 256), lambda g, t: (g, 0, 0, 0)) for rows in (rows_a, rows_b)
        ],
    )
    size = steps * 4 * (rows_a + rows_b) * 256
    return pl.pallas_call(
        down_kernel,
        grid_spec=grid_spec,
        out_shape=[
            jax.ShapeDtypeStruct((steps, 4, rows, 256), BF) for rows in (rows_a, rows_b)
        ],
        compiler_params=PARAMS,
        cost_estimate=cost(2 * size * width, 2 * size + w.size),
    )(table, hidden_a, hidden_b, w)


def add(*parts):
    total = parts[0].astype(F32)
    for part in parts[1:]:
        total = total + part.astype(F32)
    return total


def ring_scatter(kept, crossed, first, second):
    moving = add(kept[0], crossed[0]).astype(BF)
    for s in range(1, 4):
        moving = add(first(moving), kept[s], crossed[s]).astype(BF)
    return add(moving[3], *(second(moving[s], -1 - s) for s in range(3)))


def shards(
    tokens,
    norm_gain,
    base_gate,
    base_up,
    base_down,
    code_gate,
    code_up,
    scale_gate,
    scale_up,
    code_down,
    scale_down,
    cu_seqlens,
):
    capacity = tokens.shape[0]
    rows_b = capacity - HALF_A
    xl, z, y, xh, c = (lax.axis_index(a) for a in ("xl", "z", "y", "xh", "c"))
    x = xh * 2 + xl
    four = jnp.arange(4, dtype=jnp.int32)
    way = 1 - 2 * c

    turned = lax.dot_general(
        jnp.eye(32, dtype=BF), code_down, (((1,), (1,)), ((), ())), preferred_element_type=F32
    )
    deltas = to_units(
        by_units(
            scaled_rows(code_gate, scale_gate),
            scaled_rows(code_up, scale_up),
            scaled_rows(turned, scale_down.T),
        )
    )
    both_0, down_0 = deltas[:, :2], deltas[:, 2]

    later = after(tokens, both_0)
    both_1 = step_z(both_0)
    stack_a = jnp.stack(direct_gather(later[:HALF_A], step_y))
    stack_b = jnp.stack(direct_gather(later[HALF_A:], step_x))

    table = jnp.concatenate(
        [
            (z - way * four) % 4,
            (x - way * four) % 4,
            (y - way * four) % 4,
            (x + way * four) % 4,
            (y + way * four) % 4,
            jnp.stack([c, 1 - c, xl]),
        ]
    ).astype(jnp.int32)
    gain = norm_gain.reshape(norm_gain.shape[0] // 128, 128)
    width = base_gate.shape[1] // 2
    size = 4096 * width
    once = pl.Buffered(1)
    half = pl.BlockSpec((4096, width), lambda g, t: (0, t[22]), pipeline_mode=once)

    def weights_of(gate, up, deltas):
        whole = lambda a: pl.BlockSpec(a.shape, lambda g, t: (0,) * a.ndim, pipeline_mode=once)
        return pl.pallas_call(
            weights_kernel,
            grid_spec=pltpu.PrefetchScalarGridSpec(
                num_scalar_prefetch=1,
                grid=(1,),
                in_specs=[half, half, whole(gain)] + [whole(d) for d in deltas],
                out_specs=pl.BlockSpec((4096, 2 * width), lambda g, t: (0, 0), pipeline_mode=once),
            ),
            out_shape=jax.ShapeDtypeStruct((4096, 2 * width), BF),
            compiler_params=PARAMS,
            cost_estimate=cost(8 * size, 16 * size),
        )(table, gate, up, gain, *deltas)

    def round_of(mine_a, mine_b, other_a, other_b, *more):
        a, b = mine_a[-1], mine_b[-1]
        moved = [step_x(a), step_y(b), swap_cores(a), swap_cores(b)]
        moved, more = lax.optimization_barrier((moved, more))
        for pieces, piece in zip((mine_a, mine_b, other_a, other_b), moved):
            pieces.append(piece)
        return more

    stack_a, stack_b, both_1 = lax.optimization_barrier((stack_a, stack_b, both_1))
    tokens_at = ([stack_a], [stack_b], [], [])
    (both_2,) = round_of(*tokens_at, step_z(both_1))
    (both_3,) = round_of(*tokens_at, step_z(both_2))
    deltas = (both_0, both_1, both_2, both_3)
    w_both, down_1 = round_of(
        *tokens_at, weights_of(base_gate, base_up, deltas), step_z(down_0)
    )
    down_2, down_3 = step_z(down_1), step_z(down_0, 3)
    mine_a, mine_b, other_a, other_b = tokens_at
    other_a.append(swap_cores(mine_a[-1]))
    other_b.append(swap_cores(mine_b[-1]))

    anywhere = pl.BlockSpec(memory_space=pl.ANY)
    hidden_a, hidden_b = pl.pallas_call(
        hidden_kernel,
        in_specs=[SMEM] + [anywhere] * 17,
        out_specs=[VMEM] * 2,
        out_shape=[
            jax.ShapeDtypeStruct((2 * HALF_A, width), BF),
            jax.ShapeDtypeStruct((2 * rows_b, width), BF),
        ],
        scratch_shapes=[
            pltpu.VMEM((2, HALF_A, 4096), BF),
            pltpu.VMEM((2, rows_b, 4096), BF),
            pltpu.VMEM((4096, 2 * width), BF),
            pltpu.VMEM((HALF_A, 128), F32),
            pltpu.SemaphoreType.DMA((65,)),
        ],
        compiler_params=pltpu.CompilerParams(vmem_limit_bytes=60 * 1024 * 1024),
        cost_estimate=cost(8 * capacity * size, 4 * size + 4 * capacity * 4096),
    )(table, w_both, *mine_a, *other_a, *mine_b, *other_b)

    down_2, down_3 = after((down_2, down_3), (hidden_a, hidden_b))
    w_down = pl.pallas_call(
        down_weights_kernel,
        grid_spec=pltpu.PrefetchScalarGridSpec(
            num_scalar_prefetch=1,
            grid=(1,),
            in_specs=[pl.BlockSpec((width, 4096), lambda g, t: (t[22], 0), pipeline_mode=once)]
            + [pl.BlockSpec(down_0.shape, lambda g, t: (0, 0, 0), pipeline_mode=once)] * 4,
            out_specs=pl.BlockSpec(
                (2, 2, 2, 2, width, 256), lambda g, t: (0,) * 6, pipeline_mode=once
            ),
        ),
        out_shape=jax.ShapeDtypeStruct((2, 2, 2, 2, width, 256), BF),
        compiler_params=PARAMS,
        cost_estimate=cost(4 * size, 8 * size),
    )(table, base_down, down_0, down_1, down_2, down_3)

    def down_table(core):
        w = 1 - 2 * core
        return jnp.concatenate(
            [
                (x - w * (four + 1)) % 4,
                (y - w * (four + 1)) % 4,
                (w * (y - four) - 1) % 4,
                (w * (x - four) - 1) % 4,
                core[None],
            ]
        ).astype(jnp.int32)

    both = jnp.concatenate([down_table(1 - c), down_table(c)])
    partials = lambda a, chunks: down_partials(both, a, hidden_b, w_down, chunks)
    first = partials(hidden_a, [(0, 0)])
    rest = partials(after(hidden_a, first), [(0, 1), (0, 2), (0, 3)])
    kept = partials(after(hidden_a, rest), [(1, 0), (1, 1), (1, 2), (1, 3)])
    sum_a, sum_b = (
        ring_scatter(kept[k], [swap_cores(first[k])[0], *swap_cores(rest[k])], *steps)
        for k, steps in enumerate(((step_x, step_y), (step_y, step_x)))
    )
    summed = jnp.concatenate([sum_a, sum_b])

    bounds = cu_seqlens[0]
    positions = jnp.arange(capacity, dtype=jnp.int32)
    mixed = (tokens.astype(F32) + summed).astype(BF)
    mixed = jnp.where((positions < bounds[SEQS])[:, None], mixed, jnp.zeros((), BF))
    member = (positions[None, :] >= bounds[:-1, None]) & (positions[None, :] < bounds[1:, None])
    seq_sums = jnp.dot(member.astype(BF), mixed, preferred_element_type=F32)
    lengths = (bounds[1:] - bounds[:-1]).astype(F32)
    return (mixed, seq_sums / lengths[:, None])


def solution(mesh):
    torus = Mesh(mesh.devices.reshape(2, 4, 4, 2, 2), ("xl", "z", "y", "xh", "c"))
    fsdp, tp = ("xl", "z"), ("y", "xh", "c")
    both = fsdp + tp
    in_specs = (
        P(fsdp, tp),
        P(),
        P(None, tp),
        P(None, tp),
        P(tp, None),
        P(both, None),
        P(both, None),
        P(both, None),
        P(both, None),
        P(None, both),
        P(None, both),
        P(fsdp, None),
    )
    out_specs = (P(fsdp, tp), P(fsdp, tp))
    return jax.shard_map(shards, mesh=torus, in_specs=in_specs, out_specs=out_specs, check_vma=False)
```

```python
import jax
import jax.numpy as jnp
from jax import lax
from jax.experimental import pallas as pl
from jax.experimental.pallas import tpu as pltpu
from jax.sharding import Mesh
from jax.sharding import PartitionSpec as P

SEQS = 8
EPSILON = 1e-06
HALF_A = 384
PLANE = ("xl", "y", "xh", "c")
BF = jnp.bfloat16
F32 = jnp.float32
VMEM = pl.BlockSpec(memory_space=pltpu.VMEM)
SMEM = pl.BlockSpec(memory_space=pltpu.SMEM)


def ring_pairs(steps, chip_index):
    pairs = []
    for core in range(2):
        for place in range(4):
            there = (place + (steps if core == 0 else -steps)) % 4
            pairs.append((chip_index(place) * 2 + core, chip_index(there) * 2 + core))
    return pairs


def step_z(value, steps=1):
    return lax.ppermute(value, ("z", "c"), ring_pairs(steps, lambda p: p))


def step_y(value, steps=1):
    return lax.ppermute(value, ("y", "c"), ring_pairs(steps, lambda p: p))


def step_x(value, steps=1):
    order = ring_pairs(steps, lambda p: (p % 2) * 2 + p // 2)
    return lax.ppermute(value, ("xl", "xh", "c"), order)


def swap_cores(value):
    return lax.ppermute(value, "c", [(0, 1), (1, 0)])


def after(value, other):
    return lax.optimization_barrier((value, other))[0]


def ring_gather(value, step):
    pieces = [value]
    for _ in range(3):
        pieces.append(step(pieces[-1]))
    return pieces


def by_units(*deltas):
    rows, units = deltas[0].shape
    count, width = len(deltas), units // 32
    parts = [d.reshape(rows, 16, 2, width).transpose(2, 1, 0, 3) for d in deltas]
    return jnp.stack(parts, axis=2).reshape(32, count, rows, width)


def to_units(parts):
    return lax.all_to_all(parts, PLANE, split_axis=0, concat_axis=0, tiled=True)


def scaled_rows(code, scale):
    rows, units = code.shape
    blocks = scale.shape[1]
    spread = code.astype(F32).reshape(rows, blocks, units // blocks) * scale[:, :, None]
    return spread.reshape(rows, units).astype(BF)


PARAMS = pltpu.CompilerParams(vmem_limit_bytes=60 * 1024 * 1024)


def cost(flops, bytes_accessed):
    return pl.CostEstimate(flops=int(flops), bytes_accessed=int(bytes_accessed), transcendentals=0)


def weights_kernel(table, base_gate, base_up, gain, *refs):
    *deltas, out = refs
    width = base_gate.shape[1]
    for s in range(4):
        for xl in range(2):
            for k in range(4):
                at = pl.multiple_of(xl * 2048 + table[s] * 512 + k * 128, 128)
                row = gain[pl.ds(at // 128, 1), :]
                factor = jnp.broadcast_to(row, (128, 128)).T
                factor = jnp.concatenate([factor] * 3, axis=1)
                first = xl * 16 + k * 4
                for which, base in enumerate((base_gate, base_up)):
                    total = base[pl.ds(at, 128), :].astype(F32)
                    delta = deltas[which * 4 + s][first : first + 4]
                    total += delta.reshape(128, width).astype(F32)
                    total = (total * factor).astype(BF)
                    out[pl.ds(at, 128), which * width : (which + 1) * width] = total


def hidden_kernel(table, w_from, *refs):
    pieces = ((refs[0:4], refs[4:8]), (refs[8:12], refs[12:16]))
    outs, halves, (w, inverse, done) = refs[16:18], refs[18:20], refs[20:]
    width = outs[0].shape[1]
    copies = ([], [])
    for half in range(2):
        for core in range(2):
            for i in range(4):
                for j in range(4):
                    x_i, y_j = table[4 + 8 * core + i], table[8 + 8 * core + j]
                    unit = y_j * 4 + (x_i // 2) * 2 + table[20 + core]
                    group = pieces[half][core]
                    copies[half].append(
                        pltpu.make_async_copy(
                            group[j].at[i] if half else group[i].at[j],
                            halves[half].at[
                                x_i % 2, :, pl.ds(pl.multiple_of(unit * 256, 256), 256)
                            ],
                            done.at[half * 32 + core * 16 + i * 4 + j],
                        )
                    )
    weights = pltpu.make_async_copy(w_from, w, done.at[64])
    for copy in copies[0]:
        copy.start()
    weights.start()
    for copy in copies[1]:
        copy.start()
    for half in range(2):
        rows, out = halves[half], outs[half]
        count = rows.shape[1]
        for copy in copies[half]:
            copy.wait()
        for xl in range(2):
            for first in range(0, count, 64):
                last = min(first + 64, count)
                total = jnp.zeros((last - first, 128), F32)
                for k in range(16):
                    wide = rows[xl, first:last, k * 256 : (k + 1) * 256].astype(F32)
                    wide = wide * wide
                    total += wide[:, :128] + wide[:, 128:]
                mean = jnp.sum(total, axis=1, keepdims=True) * (1.0 / 4096.0)
                value = lax.rsqrt(mean + EPSILON)
                inverse[first:last, :] = jnp.broadcast_to(value, (last - first, 128))
            if half == 0 and xl == 0:
                weights.wait()
            both = jnp.dot(rows[xl], w[...], preferred_element_type=F32)
            factor = jnp.concatenate([inverse[:count, :]] * 3, axis=1)
            gate = both[:, :width] * factor
            hidden = gate / (1.0 + jnp.exp(-gate)) * (both[:, width:] * factor)
            out[xl * count : (xl + 1) * count, :] = hidden.astype(BF)


def send_kernel(table, base, d0, d1, d2, d3, hidden_a, hidden_b, w, first_a, first_b, rest_a, rest_b):
    width = base.shape[0]
    for s, delta in enumerate((d0, d1, d2, d3)):
        place = table[34 + s]
        for xl in range(2):
            for core in range(2):
                at = pl.multiple_of((xl * 8 + place * 2 + core) * 256, 256)
                first = xl * 16 + core * 8
                total = base[:, pl.ds(at, 256)].astype(F32)
                total += delta[first : first + 8].reshape(256, width).astype(F32).T
                w[xl, place // 2, place % 2, core] = total.astype(BF)
    core = table[16]
    for at in range(4):
        outs = (first_a.at[0], first_b.at[0])
        if at > 0:
            outs = (rest_a.at[at - 1], rest_b.at[at - 1])
        down_chunk(table, 0, at, hidden_a, hidden_b, w, core, *outs)


def down_chunk(table, start, at, hidden_a, hidden_b, w, core, out_a, out_b):
    rows_a, rows_b = out_a.shape[1], out_b.shape[1]
    x_i = table[start + at]
    left = hidden_a[pl.ds(pl.multiple_of((x_i % 2) * rows_a, rows_a), rows_a), :]
    right = jnp.concatenate([w[y // 2, y % 2, x_i // 2, core] for y in range(4)], axis=1)
    part_a = jnp.dot(left, right, preferred_element_type=F32).astype(BF)
    for y in range(4):
        out_a[table[start + 8 + y]] = part_a[:, y * 256 : (y + 1) * 256]
    y_j = table[start + 4 + at]
    right = jnp.concatenate([w[y_j // 2, y_j % 2, xh, core] for xh in range(2)], axis=1)
    part_b = jnp.dot(hidden_b[...], right, preferred_element_type=F32).astype(BF)
    for xh in range(2):
        for xl in range(2):
            value = part_b[xl * rows_b : (xl + 1) * rows_b, xh * 256 : (xh + 1) * 256]
            out_b[table[start + 12 + xh * 2 + xl]] = value


def keep_kernel(table, hidden_a, hidden_b, w, out_a, out_b):
    at = pl.program_id(0)
    down_chunk(table, 17, at, hidden_a, hidden_b, w, 0, out_a.at[0], out_b.at[0])


def kept_partials(table, hidden_a, hidden_b, w):
    rows = (hidden_a.shape[0] // 2, hidden_b.shape[0] // 2)
    width = hidden_a.shape[1]
    whole = lambda g, t: (0, 0)
    return pl.pallas_call(
        keep_kernel,
        grid_spec=pltpu.PrefetchScalarGridSpec(
            num_scalar_prefetch=1,
            grid=(4,),
            in_specs=[
                pl.BlockSpec(hidden_a.shape, whole),
                pl.BlockSpec(hidden_b.shape, whole),
                pl.BlockSpec((2, 2, 2, 1, width, 256), lambda g, t: (0, 0, 0, t[33], 0, 0)),
            ],
            out_specs=[pl.BlockSpec((1, 4, r, 256), lambda g, t: (g, 0, 0, 0)) for r in rows],
        ),
        out_shape=[jax.ShapeDtypeStruct((4, 4, r, 256), BF) for r in rows],
        compiler_params=PARAMS,
        cost_estimate=cost(8192 * sum(rows) * width, 8192 * sum(rows)),
    )(table, hidden_a, hidden_b, w)


def add(*parts):
    total = parts[0].astype(F32)
    for part in parts[1:]:
        total = total + part.astype(F32)
    return total


def ring_scatter(kept, crossed, first, second):
    moving = add(kept[0], crossed[0]).astype(BF)
    for s in range(1, 4):
        moving = add(first(moving), kept[s], crossed[s]).astype(BF)
    return add(moving[3], *(second(moving[s], -1 - s) for s in range(3)))


def shards(
    tokens,
    norm_gain,
    base_gate,
    base_up,
    base_down,
    code_gate,
    code_up,
    scale_gate,
    scale_up,
    code_down,
    scale_down,
    cu_seqlens,
):
    capacity = tokens.shape[0]
    rows_b = capacity - HALF_A
    xl, z, y, xh, c = (lax.axis_index(a) for a in ("xl", "z", "y", "xh", "c"))
    x = xh * 2 + xl
    four = jnp.arange(4, dtype=jnp.int32)
    way = 1 - 2 * c

    turned = lax.dot_general(
        jnp.eye(32, dtype=BF), code_down, (((1,), (1,)), ((), ())), preferred_element_type=F32
    )
    parts = by_units(scaled_rows(code_up, scale_up), scaled_rows(turned, scale_down.T))
    gate_0 = to_units(by_units(scaled_rows(code_gate, scale_gate)))[:, 0]
    gate_1, gate_3 = step_z(gate_0), step_z(gate_0, 3)
    moved = to_units(after(parts, gate_0))
    up_0, down_0 = moved[:, 0], moved[:, 1]

    later, gate_1, gate_3 = after((tokens, gate_1, gate_3), up_0)
    rows_first, rows_last = later[:HALF_A], later[HALF_A:]
    gate_2, near, up_0 = lax.optimization_barrier(
        (
            step_z(gate_1),
            [step_y(rows_first), step_x(rows_last), step_y(rows_first, 3), step_x(rows_last, 3)],
            up_0,
        )
    )
    up_1 = step_z(up_0)
    stack_a = jnp.stack([rows_first, near[0], step_y(near[0]), near[2]])
    stack_b = jnp.stack([rows_last, near[1], step_x(near[1]), near[3]])

    table = jnp.concatenate(
        [
            (z - way * four) % 4,
            (x - way * four) % 4,
            (y - way * four) % 4,
            (x + way * four) % 4,
            (y + way * four) % 4,
            jnp.stack([c, 1 - c, xl]),
        ]
    ).astype(jnp.int32)
    gain = norm_gain.reshape(norm_gain.shape[0] // 128, 128)
    width = base_gate.shape[1] // 2
    size = 4096 * width
    once = pl.Buffered(1)
    half = pl.BlockSpec((4096, width), lambda g, t: (0, t[22]), pipeline_mode=once)

    def weights_of(gate, up, deltas):
        whole = lambda a: pl.BlockSpec(a.shape, lambda g, t: (0,) * a.ndim, pipeline_mode=once)
        return pl.pallas_call(
            weights_kernel,
            grid_spec=pltpu.PrefetchScalarGridSpec(
                num_scalar_prefetch=1,
                grid=(1,),
                in_specs=[half, half, whole(gain)] + [whole(d) for d in deltas],
                out_specs=pl.BlockSpec((4096, 2 * width), lambda g, t: (0, 0), pipeline_mode=once),
            ),
            out_shape=jax.ShapeDtypeStruct((4096, 2 * width), BF),
            compiler_params=PARAMS,
            cost_estimate=cost(8 * size, 16 * size),
        )(table, gate, up, gain, *deltas)

    def round_of(mine_a, mine_b, other_a, other_b, *more):
        a, b = mine_a[-1], mine_b[-1]
        moved = [step_x(a), step_y(b), swap_cores(a), swap_cores(b)]
        moved, more = lax.optimization_barrier((moved, more))
        for pieces, piece in zip((mine_a, mine_b, other_a, other_b), moved):
            pieces.append(piece)
        return more

    stack_a, stack_b, up_0 = lax.optimization_barrier((stack_a, stack_b, up_0))
    tokens_at = ([stack_a], [stack_b], [], [])
    up_3, up_1, down_0 = round_of(*tokens_at, step_z(up_0, 3), up_1, down_0)
    up_2, down_0 = round_of(*tokens_at, step_z(up_1), down_0)
    deltas = (gate_0, gate_1, gate_2, gate_3, up_0, up_1, up_2, up_3)
    w_both, down_1 = round_of(
        *tokens_at, weights_of(base_gate, base_up, deltas), step_z(down_0)
    )
    down_2, down_3 = step_z(down_1), step_z(down_0, 3)
    mine_a, mine_b, other_a, other_b = tokens_at
    other_a.append(swap_cores(mine_a[-1]))
    other_b.append(swap_cores(mine_b[-1]))

    anywhere = pl.BlockSpec(memory_space=pl.ANY)
    hidden_a, hidden_b = pl.pallas_call(
        hidden_kernel,
        in_specs=[SMEM] + [anywhere] * 17,
        out_specs=[VMEM] * 2,
        out_shape=[
            jax.ShapeDtypeStruct((2 * HALF_A, width), BF),
            jax.ShapeDtypeStruct((2 * rows_b, width), BF),
        ],
        scratch_shapes=[
            pltpu.VMEM((2, HALF_A, 4096), BF),
            pltpu.VMEM((2, rows_b, 4096), BF),
            pltpu.VMEM((4096, 2 * width), BF),
            pltpu.VMEM((HALF_A, 128), F32),
            pltpu.SemaphoreType.DMA((65,)),
        ],
        compiler_params=pltpu.CompilerParams(vmem_limit_bytes=60 * 1024 * 1024),
        cost_estimate=cost(8 * capacity * size, 4 * size + 4 * capacity * 4096),
    )(table, w_both, *mine_a, *other_a, *mine_b, *other_b)

    def down_table(core):
        w = 1 - 2 * core
        return jnp.concatenate(
            [
                (x - w * (four + 1)) % 4,
                (y - w * (four + 1)) % 4,
                (w * (y - four) - 1) % 4,
                (w * (x - four) - 1) % 4,
                core[None],
            ]
        ).astype(jnp.int32)

    orders = jnp.concatenate([down_table(1 - c), down_table(c), (z - way * four) % 4])
    orders = orders.astype(jnp.int32)
    down_2, down_3 = after((down_2, down_3), (hidden_a, hidden_b))
    halves = (HALF_A, rows_b)
    whole = lambda shape: pl.BlockSpec(shape, lambda g, t: (0,) * len(shape), pipeline_mode=once)
    shapes = [(2, 2, 2, 2, width, 256)] + [(n, 4, r, 256) for n in (1, 3) for r in halves]
    operands = (down_0, down_1, down_2, down_3, hidden_a, hidden_b)
    w_down, *sent = pl.pallas_call(
        send_kernel,
        grid_spec=pltpu.PrefetchScalarGridSpec(
            num_scalar_prefetch=1,
            grid=(1,),
            in_specs=[pl.BlockSpec((width, 4096), lambda g, t: (t[38], 0), pipeline_mode=once)]
            + [whole(v.shape) for v in operands],
            out_specs=[whole(shape) for shape in shapes],
        ),
        out_shape=[jax.ShapeDtypeStruct(shape, BF) for shape in shapes],
        compiler_params=PARAMS,
        cost_estimate=cost(8192 * capacity * width, 8 * size + 8192 * capacity),
    )(jnp.concatenate([orders, xl[None].astype(jnp.int32)]), base_down, *operands)
    crossed = [swap_cores(v) for v in sent[:2]]
    kept = kept_partials(orders, hidden_a, hidden_b, w_down)
    rest = after(sent[2:], (crossed, kept))
    sum_a, sum_b = (
        ring_scatter(kept[k], [crossed[k][0], *swap_cores(rest[k])], *steps)
        for k, steps in enumerate(((step_x, step_y), (step_y, step_x)))
    )
    summed = jnp.concatenate([sum_a, sum_b])

    bounds = cu_seqlens[0]
    positions = jnp.arange(capacity, dtype=jnp.int32)
    mixed = (tokens.astype(F32) + summed).astype(BF)
    mixed = jnp.where((positions < bounds[SEQS])[:, None], mixed, jnp.zeros((), BF))
    member = (positions[None, :] >= bounds[:-1, None]) & (positions[None, :] < bounds[1:, None])
    seq_sums = jnp.dot(member.astype(BF), mixed, preferred_element_type=F32)
    lengths = (bounds[1:] - bounds[:-1]).astype(F32)
    return (mixed, seq_sums / lengths[:, None])


def solution(mesh):
    torus = Mesh(mesh.devices.reshape(2, 4, 4, 2, 2), ("xl", "z", "y", "xh", "c"))
    fsdp, tp = ("xl", "z"), ("y", "xh", "c")
    both = fsdp + tp
    in_specs = (
        P(fsdp, tp),
        P(),
        P(None, tp),
        P(None, tp),
        P(tp, None),
        P(both, None),
        P(both, None),
        P(both, None),
        P(both, None),
        P(None, both),
        P(None, both),
        P(fsdp, None),
    )
    out_specs = (P(fsdp, tp), P(fsdp, tp))
    return jax.shard_map(shards, mesh=torus, in_specs=in_specs, out_specs=out_specs, check_vma=False)
```

```python
import jax
import jax.numpy as jnp
from jax import lax
from jax.experimental import pallas as pl
from jax.experimental.pallas import tpu as pltpu
from jax.sharding import Mesh
from jax.sharding import PartitionSpec as P

SEQS = 8
EPSILON = 1e-06
HALF_A = 384
PLANE = ("xl", "y", "xh", "c")
BF = jnp.bfloat16
F32 = jnp.float32
VMEM = pl.BlockSpec(memory_space=pltpu.VMEM)
SMEM = pl.BlockSpec(memory_space=pltpu.SMEM)


def ring_pairs(steps, chip_index):
    pairs = []
    for core in range(2):
        for place in range(4):
            there = (place + (steps if core == 0 else -steps)) % 4
            pairs.append((chip_index(place) * 2 + core, chip_index(there) * 2 + core))
    return pairs


def step_z(value, steps=1):
    return lax.ppermute(value, ("z", "c"), ring_pairs(steps, lambda p: p))


def step_y(value, steps=1):
    return lax.ppermute(value, ("y", "c"), ring_pairs(steps, lambda p: p))


def step_x(value, steps=1):
    order = ring_pairs(steps, lambda p: (p % 2) * 2 + p // 2)
    return lax.ppermute(value, ("xl", "xh", "c"), order)


def swap_cores(value):
    return lax.ppermute(value, "c", [(0, 1), (1, 0)])


def after(value, other):
    return lax.optimization_barrier((value, other))[0]


def ring_gather(value, step):
    pieces = [value]
    for _ in range(3):
        pieces.append(step(pieces[-1]))
    return pieces


def to_units(parts):
    return lax.all_to_all(parts, PLANE, split_axis=0, concat_axis=0, tiled=True)


PARAMS = pltpu.CompilerParams(vmem_limit_bytes=60 * 1024 * 1024)


def cost(flops, bytes_accessed):
    return pl.CostEstimate(flops=int(flops), bytes_accessed=int(bytes_accessed), transcendentals=0)


def scale_kernel(*refs):
    *inputs, out = refs
    count = out.shape[1]
    for k in range(count):
        code, scale = inputs[k], inputs[count + k]
        for block in range(scale.shape[1]):
            unit, part = block // 3, block % 3
            device = (unit % 2) * 16 + unit // 2
            value = code[:, block * 128 : (block + 1) * 128].astype(F32) * scale[:, block : block + 1]
            out[device, k, :, part * 128 : (part + 1) * 128] = value.astype(BF)


def by_units(codes, scales):
    rows, units = codes[0].shape
    return pl.pallas_call(
        scale_kernel,
        in_specs=[VMEM] * (2 * len(codes)),
        out_specs=VMEM,
        out_shape=jax.ShapeDtypeStruct((32, len(codes), rows, units // 32), BF),
        compiler_params=PARAMS,
        cost_estimate=cost(len(codes) * rows * units, 4 * len(codes) * rows * units),
    )(*codes, *scales)


def weights_kernel(table, base_gate, base_up, gain, *refs):
    *deltas, out = refs
    width = base_gate.shape[1]
    for s in range(4):
        for xl in range(2):
            for k in range(4):
                at = pl.multiple_of(xl * 2048 + table[s] * 512 + k * 128, 128)
                row = gain[pl.ds(at // 128, 1), :]
                factor = jnp.broadcast_to(row, (128, 128)).T
                factor = jnp.concatenate([factor] * 3, axis=1)
                first = xl * 16 + k * 4
                for which, base in enumerate((base_gate, base_up)):
                    total = base[pl.ds(at, 128), :].astype(F32)
                    delta = deltas[which * 4 + s][first : first + 4]
                    total += delta.reshape(128, width).astype(F32)
                    total = (total * factor).astype(BF)
                    out[pl.ds(at, 128), which * width : (which + 1) * width] = total


def hidden_kernel(table, w_from, *refs):
    pieces = ((refs[0:4], refs[4:8]), (refs[8:12], refs[12:16]))
    outs, halves, (w, inverse, done) = refs[16:18], refs[18:20], refs[20:]
    width = outs[0].shape[1]
    copies = ([], [])
    for half in range(2):
        for core in range(2):
            for i in range(4):
                for j in range(4):
                    x_i, y_j = table[4 + 8 * core + i], table[8 + 8 * core + j]
                    unit = y_j * 4 + (x_i // 2) * 2 + table[20 + core]
                    group = pieces[half][core]
                    copies[half].append(
                        pltpu.make_async_copy(
                            group[j].at[i] if half else group[i].at[j],
                            halves[half].at[
                                x_i % 2, :, pl.ds(pl.multiple_of(unit * 256, 256), 256)
                            ],
                            done.at[half * 32 + core * 16 + i * 4 + j],
                        )
                    )
    weights = pltpu.make_async_copy(w_from, w, done.at[64])
    for copy in copies[0]:
        copy.start()
    weights.start()
    for copy in copies[1]:
        copy.start()
    for half in range(2):
        rows, out = halves[half], outs[half]
        count = rows.shape[1]
        for copy in copies[half]:
            copy.wait()
        for xl in range(2):
            for first in range(0, count, 64):
                last = min(first + 64, count)
                total = jnp.zeros((last - first, 128), F32)
                for k in range(16):
                    wide = rows[xl, first:last, k * 256 : (k + 1) * 256].astype(F32)
                    wide = wide * wide
                    total += wide[:, :128] + wide[:, 128:]
                mean = jnp.sum(total, axis=1, keepdims=True) * (1.0 / 4096.0)
                value = lax.rsqrt(mean + EPSILON)
                inverse[first:last, :] = jnp.broadcast_to(value, (last - first, 128))
            if half == 0 and xl == 0:
                weights.wait()
            for first in range(0, count, 192):
                last = min(first + 192, count)
                both = jnp.dot(rows[xl, first:last], w[...], preferred_element_type=F32)
                factor = jnp.concatenate([inverse[first:last, :]] * 3, axis=1)
                gate = both[:, :width] * factor
                hidden = gate / (1.0 + jnp.exp(-gate)) * (both[:, width:] * factor)
                out[xl * count + first : xl * count + last, :] = hidden.astype(BF)


def send_kernel(table, base, d0, d1, d2, d3, hidden_a, hidden_b, w, first_a, first_b, rest_a, rest_b):
    width = base.shape[0]
    for s, delta in enumerate((d0, d1, d2, d3)):
        place = table[34 + s]
        for xl in range(2):
            for core in range(2):
                at = pl.multiple_of((xl * 8 + place * 2 + core) * 256, 256)
                first = xl * 16 + core * 8
                total = base[:, pl.ds(at, 256)].astype(F32)
                total += delta[first : first + 8].reshape(256, width).astype(F32).T
                w[xl, place // 2, place % 2, core] = total.astype(BF)
    core = table[16]
    for at in range(4):
        outs = (first_a.at[0], first_b.at[0])
        if at > 0:
            outs = (rest_a.at[at - 1], rest_b.at[at - 1])
        down_chunk(table, 0, at, hidden_a, hidden_b, w, core, *outs)


def down_chunk(table, start, at, hidden_a, hidden_b, w, core, out_a, out_b):
    rows_a, rows_b = out_a.shape[1], out_b.shape[1]
    x_i = table[start + at]
    left = hidden_a[pl.ds(pl.multiple_of((x_i % 2) * rows_a, rows_a), rows_a), :]
    right = jnp.concatenate([w[y // 2, y % 2, x_i // 2, core] for y in range(4)], axis=1)
    part_a = jnp.dot(left, right, preferred_element_type=F32).astype(BF)
    for y in range(4):
        out_a[table[start + 8 + y]] = part_a[:, y * 256 : (y + 1) * 256]
    y_j = table[start + 4 + at]
    right = jnp.concatenate([w[y_j // 2, y_j % 2, xh, core] for xh in range(2)], axis=1)
    part_b = jnp.dot(hidden_b[...], right, preferred_element_type=F32).astype(BF)
    for xh in range(2):
        for xl in range(2):
            value = part_b[xl * rows_b : (xl + 1) * rows_b, xh * 256 : (xh + 1) * 256]
            out_b[table[start + 12 + xh * 2 + xl]] = value


def keep_kernel(table, hidden_a, hidden_b, w, out_a, out_b):
    at = pl.program_id(0)
    down_chunk(table, 17, at, hidden_a, hidden_b, w, 0, out_a.at[0], out_b.at[0])


def kept_partials(table, hidden_a, hidden_b, w):
    rows = (hidden_a.shape[0] // 2, hidden_b.shape[0] // 2)
    width = hidden_a.shape[1]
    whole = lambda g, t: (0, 0)
    return pl.pallas_call(
        keep_kernel,
        grid_spec=pltpu.PrefetchScalarGridSpec(
            num_scalar_prefetch=1,
            grid=(4,),
            in_specs=[
                pl.BlockSpec(hidden_a.shape, whole),
                pl.BlockSpec(hidden_b.shape, whole),
                pl.BlockSpec((2, 2, 2, 1, width, 256), lambda g, t: (0, 0, 0, t[33], 0, 0)),
            ],
            out_specs=[pl.BlockSpec((1, 4, r, 256), lambda g, t: (g, 0, 0, 0)) for r in rows],
        ),
        out_shape=[jax.ShapeDtypeStruct((4, 4, r, 256), BF) for r in rows],
        compiler_params=PARAMS,
        cost_estimate=cost(8192 * sum(rows) * width, 8192 * sum(rows)),
    )(table, hidden_a, hidden_b, w)


def add(*parts):
    total = parts[0].astype(F32)
    for part in parts[1:]:
        total = total + part.astype(F32)
    return total


def ring_scatter(kept, crossed, first, second):
    moving = add(kept[0], crossed[0]).astype(BF)
    for s in range(1, 4):
        moving = add(first(moving), kept[s], crossed[s]).astype(BF)
    return add(moving[3], *(second(moving[s], -1 - s) for s in range(3)))


def shards(
    tokens,
    norm_gain,
    base_gate,
    base_up,
    base_down,
    code_gate,
    code_up,
    scale_gate,
    scale_up,
    code_down,
    scale_down,
    cu_seqlens,
):
    capacity = tokens.shape[0]
    rows_b = capacity - HALF_A
    xl, z, y, xh, c = (lax.axis_index(a) for a in ("xl", "z", "y", "xh", "c"))
    x = xh * 2 + xl
    four = jnp.arange(4, dtype=jnp.int32)
    way = 1 - 2 * c

    turned = lax.dot_general(
        jnp.eye(32, dtype=BF), code_down, (((1,), (1,)), ((), ())), preferred_element_type=F32
    )
    parts = by_units((code_up, turned), (scale_up, scale_down.T))
    gate_0 = to_units(by_units((code_gate,), (scale_gate,)))[:, 0]
    gate_1, gate_3 = step_z(gate_0), step_z(gate_0, 3)
    moved = to_units(after(parts, gate_0))
    up_0, down_0 = moved[:, 0], moved[:, 1]

    later, gate_1, gate_3 = after((tokens, gate_1, gate_3), up_0)
    rows_first, rows_last = later[:HALF_A], later[HALF_A:]
    gate_2, near, up_0 = lax.optimization_barrier(
        (
            step_z(gate_1),
            [step_y(rows_first), step_x(rows_last), step_y(rows_first, 3), step_x(rows_last, 3)],
            up_0,
        )
    )
    up_1 = step_z(up_0)
    stack_a = jnp.stack([rows_first, near[0], step_y(near[0]), near[2]])
    stack_b = jnp.stack([rows_last, near[1], step_x(near[1]), near[3]])

    table = jnp.concatenate(
        [
            (z - way * four) % 4,
            (x - way * four) % 4,
            (y - way * four) % 4,
            (x + way * four) % 4,
            (y + way * four) % 4,
            jnp.stack([c, 1 - c, xl]),
        ]
    ).astype(jnp.int32)
    gain = norm_gain.reshape(norm_gain.shape[0] // 128, 128)
    width = base_gate.shape[1] // 2
    size = 4096 * width
    once = pl.Buffered(1)
    half = pl.BlockSpec((4096, width), lambda g, t: (0, t[22]), pipeline_mode=once)

    def weights_of(gate, up, deltas):
        whole = lambda a: pl.BlockSpec(a.shape, lambda g, t: (0,) * a.ndim, pipeline_mode=once)
        return pl.pallas_call(
            weights_kernel,
            grid_spec=pltpu.PrefetchScalarGridSpec(
                num_scalar_prefetch=1,
                grid=(1,),
                in_specs=[half, half, whole(gain)] + [whole(d) for d in deltas],
                out_specs=pl.BlockSpec((4096, 2 * width), lambda g, t: (0, 0), pipeline_mode=once),
            ),
            out_shape=jax.ShapeDtypeStruct((4096, 2 * width), BF),
            compiler_params=PARAMS,
            cost_estimate=cost(8 * size, 16 * size),
        )(table, gate, up, gain, *deltas)

    def round_of(mine_a, mine_b, other_a, other_b, *more):
        a, b = mine_a[-1], mine_b[-1]
        moved = [step_x(a), step_y(b), swap_cores(a), swap_cores(b)]
        moved, more = lax.optimization_barrier((moved, more))
        for pieces, piece in zip((mine_a, mine_b, other_a, other_b), moved):
            pieces.append(piece)
        return more

    stack_a, stack_b, up_0 = lax.optimization_barrier((stack_a, stack_b, up_0))
    tokens_at = ([stack_a], [stack_b], [], [])
    up_3, up_1, down_0 = round_of(*tokens_at, step_z(up_0, 3), up_1, down_0)
    up_2, down_0 = round_of(*tokens_at, step_z(up_1), down_0)
    deltas = (gate_0, gate_1, gate_2, gate_3, up_0, up_1, up_2, up_3)
    w_both, down_1 = round_of(
        *tokens_at, weights_of(base_gate, base_up, deltas), step_z(down_0)
    )
    down_2, down_3 = step_z(down_1), step_z(down_0, 3)
    mine_a, mine_b, other_a, other_b = tokens_at
    other_a.append(swap_cores(mine_a[-1]))
    other_b.append(swap_cores(mine_b[-1]))

    anywhere = pl.BlockSpec(memory_space=pl.ANY)
    hidden_a, hidden_b = pl.pallas_call(
        hidden_kernel,
        in_specs=[SMEM] + [anywhere] * 17,
        out_specs=[VMEM] * 2,
        out_shape=[
            jax.ShapeDtypeStruct((2 * HALF_A, width), BF),
            jax.ShapeDtypeStruct((2 * rows_b, width), BF),
        ],
        scratch_shapes=[
            pltpu.VMEM((2, HALF_A, 4096), BF),
            pltpu.VMEM((2, rows_b, 4096), BF),
            pltpu.VMEM((4096, 2 * width), BF),
            pltpu.VMEM((HALF_A, 128), F32),
            pltpu.SemaphoreType.DMA((65,)),
        ],
        compiler_params=pltpu.CompilerParams(vmem_limit_bytes=60 * 1024 * 1024),
        cost_estimate=cost(8 * capacity * size, 4 * size + 4 * capacity * 4096),
    )(table, w_both, *mine_a, *other_a, *mine_b, *other_b)

    def down_table(core):
        w = 1 - 2 * core
        return jnp.concatenate(
            [
                (x - w * (four + 1)) % 4,
                (y - w * (four + 1)) % 4,
                (w * (y - four) - 1) % 4,
                (w * (x - four) - 1) % 4,
                core[None],
            ]
        ).astype(jnp.int32)

    orders = jnp.concatenate([down_table(1 - c), down_table(c), (z - way * four) % 4])
    orders = orders.astype(jnp.int32)
    down_2, down_3 = after((down_2, down_3), (hidden_a, hidden_b))
    halves = (HALF_A, rows_b)
    whole = lambda shape: pl.BlockSpec(shape, lambda g, t: (0,) * len(shape), pipeline_mode=once)
    shapes = [(2, 2, 2, 2, width, 256)] + [(n, 4, r, 256) for n in (1, 3) for r in halves]
    operands = (down_0, down_1, down_2, down_3, hidden_a, hidden_b)
    w_down, *sent = pl.pallas_call(
        send_kernel,
        grid_spec=pltpu.PrefetchScalarGridSpec(
            num_scalar_prefetch=1,
            grid=(1,),
            in_specs=[pl.BlockSpec((width, 4096), lambda g, t: (t[38], 0), pipeline_mode=once)]
            + [whole(v.shape) for v in operands],
            out_specs=[whole(shape) for shape in shapes],
        ),
        out_shape=[jax.ShapeDtypeStruct(shape, BF) for shape in shapes],
        compiler_params=PARAMS,
        cost_estimate=cost(8192 * capacity * width, 8 * size + 8192 * capacity),
    )(jnp.concatenate([orders, xl[None].astype(jnp.int32)]), base_down, *operands)
    crossed = [swap_cores(v) for v in sent[:2]]
    kept = kept_partials(orders, hidden_a, hidden_b, w_down)
    rest = after(sent[2:], (crossed, kept))
    sum_a, sum_b = (
        ring_scatter(kept[k], [crossed[k][0], *swap_cores(rest[k])], *steps)
        for k, steps in enumerate(((step_x, step_y), (step_y, step_x)))
    )
    summed = jnp.concatenate([sum_a, sum_b])

    bounds = cu_seqlens[0]
    positions = jnp.arange(capacity, dtype=jnp.int32)
    mixed = (tokens.astype(F32) + summed).astype(BF)
    mixed = jnp.where((positions < bounds[SEQS])[:, None], mixed, jnp.zeros((), BF))
    member = (positions[None, :] >= bounds[:-1, None]) & (positions[None, :] < bounds[1:, None])
    seq_sums = jnp.dot(member.astype(BF), mixed, preferred_element_type=F32)
    lengths = (bounds[1:] - bounds[:-1]).astype(F32)
    return (mixed, seq_sums / lengths[:, None])


def solution(mesh):
    torus = Mesh(mesh.devices.reshape(2, 4, 4, 2, 2), ("xl", "z", "y", "xh", "c"))
    fsdp, tp = ("xl", "z"), ("y", "xh", "c")
    both = fsdp + tp
    in_specs = (
        P(fsdp, tp),
        P(),
        P(None, tp),
        P(None, tp),
        P(tp, None),
        P(both, None),
        P(both, None),
        P(both, None),
        P(both, None),
        P(None, both),
        P(None, both),
        P(fsdp, None),
    )
    out_specs = (P(fsdp, tp), P(fsdp, tp))
    return jax.shard_map(shards, mesh=torus, in_specs=in_specs, out_specs=out_specs, check_vma=False)
```
